32 devices in a mesh: dp: 2 (over x), tp: 16 (over z, y, core).
Axes of the slice: x: 2, y: 2, z: 4, core: 2. Of those that a mesh axis runs over, the one named last changes fastest.
Arguments:
- hidden: bfloat16 [512, 26624], P('dp', 'tp'), may hold values from -0.25 to 0.25
- out_grad: bfloat16 [512, 8192], P(('dp', 'tp')), may hold values from -6 to 6
- down_weight: bfloat16 [26624, 8192], P('tp', 'dp'), may hold values from -0.0625 to 0.0625
Outputs:
- input_grad: bfloat16 [512, 26624], P('dp', 'tp')
- weight_grad: bfloat16 [26624, 8192], P('tp', 'dp')
The draws below stay inside these ranges and needn't reach their ends.
All inputs are finite; a program needn't handle non-finite values.
Results may differ from the reference program's by a relative error of at most 0.009.
Values may be sent and summed in bfloat16 or wider, within the bound.
A program may use at most 128 MiB of HBM per device.

```python
import jax
import jax.numpy as jnp

D = 8192
FF = 26624
TOK_DEV = 256
TOKENS = 512
N_DP = 2


def block_levels(key, shape, cuts, low, top_value):
    gain = 1.0
    for dim, blocks in cuts:
        draws = jax.random.uniform(jax.random.fold_in(jax.random.fold_in(key, 6), dim), (blocks,), jnp.float32, low / len(cuts), top_value / len(cuts))
        gain = gain * jnp.repeat(jnp.exp(draws), shape[dim] // blocks).reshape((-1,) + (1,) * (len(shape) - 1 - dim))
    return gain


def scatter_about(stream_key, shape, width, bound, pieces=(), dtype=jnp.bfloat16):
    result = jax.random.normal(stream_key, shape, jnp.float32) * width
    if len(pieces) > 0:
        result = block_levels(stream_key, shape, pieces, -0.22, 0.18) * result
    return jnp.clip(result, min=-bound, max=bound).astype(dtype)


def setup_inputs(seed: int = 0) -> dict:
    key_of = jax.random.split(jax.random.key(seed), 4)
    hidden = scatter_about(key_of[0], (TOKENS, FF), TOKENS ** -0.5, 0.25, ((0, 2), (1, 16)))
    out_grad = scatter_about(key_of[1], (TOKENS, D), 1.0, 6.0, ((0, 32),))
    down_weight = scatter_about(key_of[2], (FF, D), D ** -0.5, 0.0625, ((0, 16), (1, 2)))
    return dict(hidden=hidden, out_grad=out_grad, down_weight=down_weight)


def reference(hidden, out_grad, down_weight):
    input_grad = jnp.dot(out_grad, down_weight.T, preferred_element_type=jnp.float32).astype(jnp.bfloat16)
    summed = jnp.zeros((FF, D), jnp.float32)
    for group in range(N_DP):
        first = group * TOK_DEV
        hidden_group = hidden[first:first + TOK_DEV]
        grad_group = out_grad[first:first + TOK_DEV]
        partial_grad = jnp.dot(hidden_group.T, grad_group, preferred_element_type=jnp.float32).astype(jnp.bfloat16)
        summed = summed + partial_grad.astype(jnp.float32)
    return input_grad, summed.astype(jnp.bfloat16)
```

```python
import jax
import jax.numpy as jnp
from jax import lax
from jax.sharding import PartitionSpec as P


def shards(hidden, out_grad, down_weight):
    own = lax.all_to_all(out_grad, "dp", split_axis=1, concat_axis=0, tiled=True)
    dp = lax.axis_size("dp")
    own = own.reshape(dp, out_grad.shape[0], own.shape[1])
    grads = lax.all_gather(own, "tp", axis=1, tiled=True)
    grads = grads.reshape(-1, grads.shape[2])
    hidden_all = lax.all_gather(hidden, "dp", axis=0, tiled=True)
    partial = lax.dot_general(
        grads, down_weight, (((1,), (1,)), ((), ())), preferred_element_type=jnp.float32
    )
    input_grad = lax.psum_scatter(partial, "dp", scatter_dimension=0, tiled=True)
    weight_grad = lax.dot_general(
        hidden_all, grads, (((0,), (0,)), ((), ())), preferred_element_type=jnp.float32
    )
    return (input_grad.astype(jnp.bfloat16), weight_grad.astype(jnp.bfloat16))


def solution(mesh):
    placed = (P("dp", "tp"), P(("dp", "tp"), None), P("tp", "dp"))
    return jax.shard_map(
        shards,
        mesh=mesh,
        in_specs=placed,
        out_specs=(P("dp", "tp"), P("tp", "dp")),
        check_vma=False,
    )
```

```python
import functools

import jax
import jax.numpy as jnp
from jax import lax
from jax.experimental import pallas as pl
from jax.experimental.pallas import tpu as pltpu
from jax.sharding import PartitionSpec as P

CORES = 2
ROWS = 2
WIDE = 256
HID_PARTS = 4
X, UP, DOWN, Y, CORE = range(5)


def gather_kernel(tp, hid, og, w, grads, hid_all, part_other, part_own,
                  og_s, w_s, pb_s, pf_s,
                  send, recv, hsend, hrecv, local, wsem, gsem):
    i = lax.axis_index("dp")
    j = lax.axis_index("tp")
    depth = tp // (CORES * ROWS)
    c = lax.rem(j, CORES)
    y = lax.rem(j // CORES, ROWS)
    z = j // (CORES * ROWS)
    other = 1 - i
    tok = hid.shape[0]
    units = w.shape[0]
    half = w.shape[1]
    rows = og.shape[0]

    def index(zz, yy, cc):
        return (zz * ROWS + yy) * CORES + cc

    places = {
        X: (other, j),
        UP: (i, index(z + 1, y, c)),
        DOWN: (i, index(z - 1, y, c)),
        Y: (i, index(z, 1 - y, c)),
        CORE: (i, index(z, y, 1 - c)),
    }
    has = {UP: z < depth - 1, DOWN: z > 0}

    def guarded(way, f):
        if way in has:
            pl.when(has[way])(f)
        else:
            f()

    starts = list(range(0, units, WIDE))
    w_copies = []
    for k, s in enumerate(starts):
        n = min(WIDE, units - s)
        w_copies.append(pltpu.make_async_copy(
            w.at[pl.ds(s, n), :], w_s.at[pl.ds(s, n), :], wsem.at[k]))
        w_copies[-1].start()
    mine = pl.ds(pl.multiple_of(i * half, 128), half)
    theirs = pl.ds(pl.multiple_of(other * half, 128), half)
    own_og = pltpu.make_async_copy(og.at[:, mine], og_s.at[i, j], local.at[0])
    own_og.start()
    own_rows = pl.ds(pl.multiple_of(i * tok, 128), tok)
    own_hid = pltpu.make_async_copy(hid, hid_all.at[own_rows, :], local.at[1])
    own_hid.start()

    barrier = pltpu.get_barrier_semaphore()
    for way in (X, UP, DOWN, Y, CORE):
        def greet(way=way):
            pl.semaphore_signal(barrier, inc=1, device_id=places[way],
                                device_id_type=pl.DeviceIdType.MESH)
        guarded(way, greet)
    pl.semaphore_wait(barrier, 3 + jnp.where(z < depth - 1, 1, 0) + jnp.where(z > 0, 1, 0))

    cross = pltpu.make_async_remote_copy(
        og.at[:, theirs], og_s.at[i, j], send.at[X, i, j], recv.at[i, j],
        device_id=places[X], device_id_type=pl.DeviceIdType.MESH)
    cross.start()
    step = tok // HID_PARTS
    hid_copies = []
    for k in range(HID_PARTS):
        at = pl.ds(pl.multiple_of(i * tok + k * step, 16), step)
        hid_copies.append(pltpu.make_async_remote_copy(
            hid.at[pl.ds(k * step, step), :], hid_all.at[at, :], hsend.at[k], hrecv.at[k],
            device_id=places[X], device_id_type=pl.DeviceIdType.MESH))
        hid_copies[-1].start()

    def block_copy(way, g, t):
        return pltpu.make_async_remote_copy(
            og_s.at[g, t], og_s.at[g, t], send.at[way, g, t], recv.at[g, t],
            device_id=places[way], device_id_type=pl.DeviceIdType.MESH)

    def keep(g, t):
        rows_at = pl.ds(pl.multiple_of((g * tp + t) * rows, 16), rows)
        return pltpu.make_async_copy(og_s.at[g, t], grads.at[rows_at, :], gsem.at[g, t])

    def arrived(g, t):
        block_copy(CORE, g, t).wait_recv()

    def pass_on(g, t, ways):
        for way in ways:
            guarded(way, lambda way=way: block_copy(way, g, t).start())
        keep(g, t).start()

    def hops(g):
        def own():
            pass_on(g, j, (UP, DOWN, Y, CORE))

        def along(s):
            def below():
                t = index(z - s, y, c)
                arrived(g, t)
                pass_on(g, t, (UP, Y, CORE))

            def above():
                t = index(z + s, y, c)
                arrived(g, t)
                pass_on(g, t, (DOWN, Y, CORE))

            pl.when(z - s >= 0)(below)
            pl.when(z + s < depth)(above)

        def across(s):
            def one(zz):
                t = index(zz, 1 - y, c)
                arrived(g, t)
                pass_on(g, t, (CORE,))

            if s == 0:
                one(z)
            else:
                pl.when(z - s >= 0)(lambda: one(z - s))
                pl.when(z + s < depth)(lambda: one(z + s))

        steps = [own]
        for s in range(1, depth):
            steps.append(functools.partial(along, s))
            steps.append(functools.partial(across, s - 1))
        steps.append(functools.partial(across, depth - 1))
        return steps

    def from_core(g):
        @pl.loop(0, depth * ROWS)
        def _(k):
            t = k * CORES + 1 - c
            arrived(g, t)
            keep(g, t).start()

    def multiply(g, k, store):
        s = starts[k]
        n = min(WIDE, units - s)
        if waited[k] == 0:
            w_copies[k].wait()
            waited[k] = 1
        lhs = og_s[g].reshape(tp * rows, half)
        store(s, n, lax.dot_general(lhs, w_s[pl.ds(s, n), :], (((1,), (1,)), ((), ())),
                                    preferred_element_type=jnp.float32))

    waited = [0] * len(starts)
    own_og.wait()
    own_steps = hops(i)
    own_steps[0]()
    arrived(other, j)
    for f in hops(other):
        f()
    from_core(other)

    def store_other(s, n, v):
        pb_s[:, pl.ds(s, n)] = v.astype(jnp.bfloat16)

    def store_own(s, n, v):
        pf_s[:, pl.ds(s, n)] = v

    rest = own_steps[1:]
    for k in range(max(len(starts), len(rest))):
        if k < len(starts):
            multiply(other, k, store_other)
        if k < len(rest):
            rest[k]()
    out_other = pltpu.make_async_copy(pb_s, part_other, local.at[2])
    out_other.start()
    from_core(i)
    for k in range(len(starts)):
        multiply(i, k, store_own)
    out_own = pltpu.make_async_copy(pf_s, part_own, local.at[3])
    out_own.start()

    cross.wait_send()
    for copy in hid_copies:
        copy.wait()

    @pl.loop(0, CORES * depth * ROWS)
    def _(t):
        for g in range(2):
            keep(g, t).wait()
    for g in (0, 1):
        @pl.loop(0, depth)
        def _(zz, g=g):
            t = index(zz, y, c)
            pl.when((zz <= z) & (z < depth - 1))(lambda: block_copy(UP, g, t).wait_send())
            pl.when((zz >= z) & (z > 0))(lambda: block_copy(DOWN, g, t).wait_send())
            block_copy(Y, g, t).wait_send()
            block_copy(CORE, g, t).wait_send()
            block_copy(CORE, g, index(zz, 1 - y, c)).wait_send()
    own_hid.wait()
    out_other.wait()
    out_own.wait()


def gather(hidden, out_grad, down_weight, tp):
    tok, units = hidden.shape
    half = down_weight.shape[1]
    rows = out_grad.shape[0]
    dma = pltpu.SemaphoreType.DMA
    anyspace = pl.BlockSpec(memory_space=pl.ANY)
    return pl.pallas_call(
        functools.partial(gather_kernel, tp),
        out_shape=(
            jax.ShapeDtypeStruct((2 * tok, half), jnp.bfloat16),
            jax.ShapeDtypeStruct((2 * tok, units), jnp.bfloat16),
            jax.ShapeDtypeStruct((tok, units), jnp.bfloat16),
            jax.ShapeDtypeStruct((tok, units), jnp.float32),
        ),
        in_specs=[anyspace] * 3,
        out_specs=[anyspace] * 4,
        scratch_shapes=[
            pltpu.VMEM((2, tp, rows, half), jnp.bfloat16),
            pltpu.VMEM((units, half), jnp.bfloat16),
            pltpu.VMEM((tok, units), jnp.bfloat16),
            pltpu.VMEM((tok, units), jnp.float32),
            dma((5, 2, tp)),
            dma((2, tp)),
            dma((HID_PARTS,)),
            dma((HID_PARTS,)),
            dma((4,)),
            dma((pl.cdiv(units, WIDE),)),
            dma((2, tp)),
        ],
        compiler_params=pltpu.CompilerParams(
            collective_id=0, has_side_effects=True, vmem_limit_bytes=48 * 2**20),
    )(hidden, out_grad, down_weight)


def shards(hidden, out_grad, down_weight):
    dp = lax.axis_size("dp")
    tp = lax.axis_size("tp")
    grads, hidden_all, part_other, part_own = gather(hidden, out_grad, down_weight, tp)
    received = lax.ppermute(part_other, "dp", [(k, 1 - k) for k in range(dp)])
    weight_grad = lax.dot_general(
        hidden_all, grads, (((0,), (0,)), ((), ())), preferred_element_type=jnp.float32
    ).astype(jnp.bfloat16)
    input_grad = (part_own + received.astype(jnp.float32)).astype(jnp.bfloat16)
    return (input_grad, weight_grad)


def plain_shards(hidden, out_grad, down_weight):
    own = lax.all_to_all(out_grad, "dp", split_axis=1, concat_axis=0, tiled=True)
    dp = lax.axis_size("dp")
    own = own.reshape(dp, out_grad.shape[0], own.shape[1])
    grads = lax.all_gather(own, "tp", axis=1, tiled=True)
    grads = grads.reshape(-1, grads.shape[2])
    hidden_all = lax.all_gather(hidden, "dp", axis=0, tiled=True)
    partial = lax.dot_general(
        grads, down_weight, (((1,), (1,)), ((), ())), preferred_element_type=jnp.float32
    )
    input_grad = lax.psum_scatter(partial, "dp", scatter_dimension=0, tiled=True)
    weight_grad = lax.dot_general(
        hidden_all, grads, (((0,), (0,)), ((), ())), preferred_element_type=jnp.float32
    )
    return (input_grad.astype(jnp.bfloat16), weight_grad.astype(jnp.bfloat16))


def choose(dp, tp, hidden, out_grad, down_weight):
    def run(hidden, out_grad, down_weight):
        rows = out_grad.shape[0]
        fits = (
            dp == 2 and tp % (CORES * ROWS) == 0 and rows % 16 == 0
            and hidden.shape[0] % (16 * HID_PARTS) == 0
            and hidden.shape[1] % 128 == 0 and down_weight.shape[1] % 128 == 0
        )
        return (shards if fits else plain_shards)(hidden, out_grad, down_weight)
    return run(hidden, out_grad, down_weight)


def solution(mesh):
    placed = (P("dp", "tp"), P(("dp", "tp"), None), P("tp", "dp"))
    return jax.shard_map(
        functools.partial(choose, mesh.shape["dp"], mesh.shape["tp"]),
        mesh=mesh,
        in_specs=placed,
        out_specs=(P("dp", "tp"), P("tp", "dp")),
        check_vma=False,
    )
```

```python
import functools

import jax
import jax.numpy as jnp
from jax import lax
from jax.experimental import pallas as pl
from jax.experimental.pallas import tpu as pltpu
from jax.sharding import PartitionSpec as P

CORES = 2
ROWS = 2
WIDE = 256
HID_PARTS = 4
SENT = 3
LEAD = 3
LAG = 2
TILE = 512
X, UP, DOWN, Y, CORE = range(5)


def gather_kernel(tp, sent, hid, og, w, grads, hid_all, part_other, part_here, part_own,
                  og_s, w_s, pb_s, pf_s,
                  send, recv, hsend, hrecv, psend, precv, local, wsem, gsem):
    i = lax.axis_index("dp")
    j = lax.axis_index("tp")
    depth = tp // (CORES * ROWS)
    c = lax.rem(j, CORES)
    y = lax.rem(j // CORES, ROWS)
    z = j // (CORES * ROWS)
    other = 1 - i
    tok = hid.shape[0]
    units = w.shape[0]
    half = w.shape[1]
    rows = og.shape[0]

    def index(zz, yy, cc):
        return (zz * ROWS + yy) * CORES + cc

    places = {
        X: (other, j),
        UP: (i, index(z + 1, y, c)),
        DOWN: (i, index(z - 1, y, c)),
        Y: (i, index(z, 1 - y, c)),
        CORE: (i, index(z, y, 1 - c)),
    }
    has = {UP: z < depth - 1, DOWN: z > 0}

    def guarded(way, f):
        if way in has:
            pl.when(has[way])(f)
        else:
            f()

    starts = list(range(0, units, WIDE))
    w_copies = []
    for k, s in enumerate(starts):
        n = min(WIDE, units - s)
        w_copies.append(pltpu.make_async_copy(
            w.at[pl.ds(s, n), :], w_s.at[pl.ds(s, n), :], wsem.at[k]))
        w_copies[-1].start()
    mine = pl.ds(pl.multiple_of(i * half, 128), half)
    theirs = pl.ds(pl.multiple_of(other * half, 128), half)
    own_og = pltpu.make_async_copy(og.at[:, mine], og_s.at[i, j], local.at[0])
    own_og.start()
    own_rows = pl.ds(pl.multiple_of(i * tok, 128), tok)
    own_hid = pltpu.make_async_copy(hid, hid_all.at[own_rows, :], local.at[1])
    own_hid.start()

    barrier = pltpu.get_barrier_semaphore()
    for way in (X, UP, DOWN, Y, CORE):
        def greet(way=way):
            pl.semaphore_signal(barrier, inc=1, device_id=places[way],
                                device_id_type=pl.DeviceIdType.MESH)
        guarded(way, greet)
    pl.semaphore_wait(barrier, 3 + jnp.where(z < depth - 1, 1, 0) + jnp.where(z > 0, 1, 0))

    cross = pltpu.make_async_remote_copy(
        og.at[:, theirs], og_s.at[i, j], send.at[X, i, j], recv.at[i, j],
        device_id=places[X], device_id_type=pl.DeviceIdType.MESH)
    cross.start()
    step = tok // HID_PARTS
    hid_copies = []
    for k in range(HID_PARTS):
        at = pl.ds(pl.multiple_of(i * tok + k * step, 16), step)
        hid_copies.append(pltpu.make_async_remote_copy(
            hid.at[pl.ds(k * step, step), :], hid_all.at[at, :], hsend.at[k], hrecv.at[k],
            device_id=places[X], device_id_type=pl.DeviceIdType.MESH))
        hid_copies[-1].start()

    def block_copy(way, g, t):
        return pltpu.make_async_remote_copy(
            og_s.at[g, t], og_s.at[g, t], send.at[way, g, t], recv.at[g, t],
            device_id=places[way], device_id_type=pl.DeviceIdType.MESH)

    def keep(g, t):
        rows_at = pl.ds(pl.multiple_of((g * tp + t) * rows, 16), rows)
        return pltpu.make_async_copy(og_s.at[g, t], grads.at[rows_at, :], gsem.at[g, t])

    def arrived(g, t):
        block_copy(CORE, g, t).wait_recv()

    def pass_on(g, t, ways):
        for way in ways:
            guarded(way, lambda way=way: block_copy(way, g, t).start())
        keep(g, t).start()

    def hops(g):
        def own():
            pass_on(g, j, (UP, DOWN, Y, CORE))

        def along(s):
            def below():
                t = index(z - s, y, c)
                arrived(g, t)
                pass_on(g, t, (UP, Y, CORE))

            def above():
                t = index(z + s, y, c)
                arrived(g, t)
                pass_on(g, t, (DOWN, Y, CORE))

            pl.when(z - s >= 0)(below)
            pl.when(z + s < depth)(above)

        def across(s):
            def one(zz):
                t = index(zz, 1 - y, c)
                arrived(g, t)
                pass_on(g, t, (CORE,))

            if s == 0:
                one(z)
            else:
                pl.when(z - s >= 0)(lambda: one(z - s))
                pl.when(z + s < depth)(lambda: one(z + s))

        steps = [own]
        for s in range(1, depth):
            steps.append(functools.partial(along, s))
            steps.append(functools.partial(across, s - 1))
        steps.append(functools.partial(across, depth - 1))
        return steps

    def from_core(g):
        @pl.loop(0, depth * ROWS)
        def _(k):
            t = k * CORES + 1 - c
            arrived(g, t)
            keep(g, t).start()

    def multiply(g, k, store):
        s = starts[k]
        n = min(WIDE, units - s)
        if waited[k] == 0:
            w_copies[k].wait()
            waited[k] = 1
        lhs = og_s[g].reshape(tp * rows, half)
        store(s, n, lax.dot_general(lhs, w_s[pl.ds(s, n), :], (((1,), (1,)), ((), ())),
                                    preferred_element_type=jnp.float32))

    waited = [0] * len(starts)
    own_og.wait()
    own_steps = hops(i)
    own_steps[0]()
    arrived(other, j)
    other_steps = hops(other)
    other_steps[0]()
    count = len(own_steps)
    for k in range(1, LEAD):
        own_steps[k]()
        other_steps[k]()
    for k in range(LEAD, count):
        other_steps[k]()
        if k < count - LAG:
            own_steps[k]()
    from_core(other)

    def store_other(s, n, v):
        pb_s[:, pl.ds(s, n)] = v.astype(jnp.bfloat16)

    def store_own(s, n, v):
        pf_s[:, pl.ds(s, n)] = v

    rest = own_steps[max(LEAD, count - LAG):]
    swaps = []
    for k in range(max(len(starts), len(rest))):
        if k < len(starts):
            multiply(other, k, store_other)
            if k < sent:
                cols = pl.ds(k * WIDE, WIDE)
                swaps.append(pltpu.make_async_remote_copy(
                    pb_s.at[:, cols], part_here.at[:, cols], psend.at[k], precv.at[k],
                    device_id=places[X], device_id_type=pl.DeviceIdType.MESH))
                swaps[-1].start()
        if k < len(rest):
            rest[k]()
    out_other = pltpu.make_async_copy(
        pb_s.at[:, pl.ds(sent * WIDE, units - sent * WIDE)], part_other, local.at[2])
    out_other.start()
    from_core(i)
    for k in range(len(starts)):
        multiply(i, k, store_own)
    out_own = pltpu.make_async_copy(pf_s, part_own, local.at[3])
    out_own.start()

    cross.wait_send()
    for copy in hid_copies + swaps:
        copy.wait()

    @pl.loop(0, CORES * depth * ROWS)
    def _(t):
        for g in range(2):
            keep(g, t).wait()
    for g in (0, 1):
        @pl.loop(0, depth)
        def _(zz, g=g):
            t = index(zz, y, c)
            pl.when((zz <= z) & (z < depth - 1))(lambda: block_copy(UP, g, t).wait_send())
            pl.when((zz >= z) & (z > 0))(lambda: block_copy(DOWN, g, t).wait_send())
            block_copy(Y, g, t).wait_send()
            block_copy(CORE, g, t).wait_send()
            block_copy(CORE, g, index(zz, 1 - y, c)).wait_send()
    own_hid.wait()
    out_other.wait()
    out_own.wait()


def gather(hidden, out_grad, down_weight, tp):
    tok, units = hidden.shape
    half = down_weight.shape[1]
    rows = out_grad.shape[0]
    dma = pltpu.SemaphoreType.DMA
    sent = max(1, units // WIDE * SENT // 6)
    anyspace = pl.BlockSpec(memory_space=pl.ANY)
    return pl.pallas_call(
        functools.partial(gather_kernel, tp, sent),
        out_shape=(
            jax.ShapeDtypeStruct((2 * tok, half), jnp.bfloat16),
            jax.ShapeDtypeStruct((2 * tok, units), jnp.bfloat16),
            jax.ShapeDtypeStruct((tok, units - sent * WIDE), jnp.bfloat16),
            jax.ShapeDtypeStruct((tok, sent * WIDE), jnp.bfloat16),
            jax.ShapeDtypeStruct((tok, units), jnp.float32),
        ),
        in_specs=[anyspace] * 3,
        out_specs=[anyspace] * 5,
        scratch_shapes=[
            pltpu.VMEM((2, tp, rows, half), jnp.bfloat16),
            pltpu.VMEM((units, half), jnp.bfloat16),
            pltpu.VMEM((tok, units), jnp.bfloat16),
            pltpu.VMEM((tok, units), jnp.float32),
            dma((5, 2, tp)),
            dma((2, tp)),
            dma((HID_PARTS,)),
            dma((HID_PARTS,)),
            dma((sent,)),
            dma((sent,)),
            dma((4,)),
            dma((pl.cdiv(units, WIDE),)),
            dma((2, tp)),
        ],
        compiler_params=pltpu.CompilerParams(
            collective_id=0, has_side_effects=True, vmem_limit_bytes=60 * 2**20),
    )(hidden, out_grad, down_weight)


def weight_kernel(h, g, out, ht):
    @pl.when(pl.program_id(0) == 0)
    def _():
        ht[...] = h[...].T

    out[...] = jnp.dot(ht[...], g[...], preferred_element_type=jnp.float32).astype(out.dtype)


def weight_gradient(hidden_all, grads):
    tokens, units = hidden_all.shape
    half = grads.shape[1]
    tile = TILE if half % TILE == 0 else 128
    return pl.pallas_call(
        weight_kernel,
        grid=(half // tile,),
        out_shape=jax.ShapeDtypeStruct((units, half), jnp.bfloat16),
        in_specs=[
            pl.BlockSpec((tokens, units), lambda n: (0, 0)),
            pl.BlockSpec((tokens, tile), lambda n: (0, n)),
        ],
        out_specs=pl.BlockSpec((units, tile), lambda n: (0, n)),
        scratch_shapes=[pltpu.VMEM((units, tokens), jnp.bfloat16)],
        compiler_params=pltpu.CompilerParams(vmem_limit_bytes=56 * 2**20),
        cost_estimate=pl.CostEstimate(
            flops=2 * tokens * units * half,
            bytes_accessed=2 * (tokens * (units + half) + units * half),
            transcendentals=0),
    )(hidden_all, grads)


def shards(hidden, out_grad, down_weight):
    dp = lax.axis_size("dp")
    tp = lax.axis_size("tp")
    grads, hidden_all, part_other, part_here, part_own = gather(
        hidden, out_grad, down_weight, tp)
    received = lax.ppermute(part_other, "dp", [(k, 1 - k) for k in range(dp)])
    weight_grad = weight_gradient(hidden_all, grads)
    received = jnp.concatenate([part_here, received], axis=1)
    input_grad = (part_own + received.astype(jnp.float32)).astype(jnp.bfloat16)
    return (input_grad, weight_grad)


def plain_shards(hidden, out_grad, down_weight):
    own = lax.all_to_all(out_grad, "dp", split_axis=1, concat_axis=0, tiled=True)
    dp = lax.axis_size("dp")
    own = own.reshape(dp, out_grad.shape[0], own.shape[1])
    grads = lax.all_gather(own, "tp", axis=1, tiled=True)
    grads = grads.reshape(-1, grads.shape[2])
    hidden_all = lax.all_gather(hidden, "dp", axis=0, tiled=True)
    partial = lax.dot_general(
        grads, down_weight, (((1,), (1,)), ((), ())), preferred_element_type=jnp.float32
    )
    input_grad = lax.psum_scatter(partial, "dp", scatter_dimension=0, tiled=True)
    weight_grad = lax.dot_general(
        hidden_all, grads, (((0,), (0,)), ((), ())), preferred_element_type=jnp.float32
    )
    return (input_grad.astype(jnp.bfloat16), weight_grad.astype(jnp.bfloat16))


def choose(dp, tp, hidden, out_grad, down_weight):
    def run(hidden, out_grad, down_weight):
        rows = out_grad.shape[0]
        fits = (
            dp == 2 and tp % (CORES * ROWS) == 0 and rows % 16 == 0
            and hidden.shape[0] % (16 * HID_PARTS) == 0
            and hidden.shape[1] % 128 == 0 and down_weight.shape[1] % 128 == 0
        )
        return (shards if fits else plain_shards)(hidden, out_grad, down_weight)
    return run(hidden, out_grad, down_weight)


def solution(mesh):
    placed = (P("dp", "tp"), P(("dp", "tp"), None), P("tp", "dp"))
    return jax.shard_map(
        functools.partial(choose, mesh.shape["dp"], mesh.shape["tp"]),
        mesh=mesh,
        in_specs=placed,
        out_specs=(P("dp", "tp"), P("tp", "dp")),
        check_vma=False,
    )
```

```python
import functools

import jax
import jax.numpy as jnp
from jax import lax
from jax.experimental import pallas as pl
from jax.experimental.pallas import tpu as pltpu
from jax.sharding import PartitionSpec as P

CORES = 2
ROWS = 2
WIDE = 256
HID_PARTS = 4
TILE = 512
X, UP, DOWN, Y, CORE = range(5)


def gather_kernel(tp, hid, og, w, grads, hid_all, part_other, part_here, part_own,
                  og_s, w_s, pb_s,
                  send, recv, hsend, hrecv, psend, precv, local, wsem, gsem):
    i = lax.axis_index("dp")
    j = lax.axis_index("tp")
    depth = tp // (CORES * ROWS)
    c = lax.rem(j, CORES)
    y = lax.rem(j // CORES, ROWS)
    z = j // (CORES * ROWS)
    other = 1 - i
    tok = hid.shape[0]
    units = w.shape[0]
    half = w.shape[1]
    rows = og.shape[0]

    def index(zz, yy, cc):
        return (zz * ROWS + yy) * CORES + cc

    places = {
        X: (other, j),
        UP: (i, index(z + 1, y, c)),
        DOWN: (i, index(z - 1, y, c)),
        Y: (i, index(z, 1 - y, c)),
        CORE: (i, index(z, y, 1 - c)),
    }
    has = {UP: z < depth - 1, DOWN: z > 0}

    def guarded(way, f):
        if way in has:
            pl.when(has[way])(f)
        else:
            f()

    starts = list(range(0, units, WIDE))
    w_copies = []
    for k, s in enumerate(starts):
        n = min(WIDE, units - s)
        w_copies.append(pltpu.make_async_copy(
            w.at[pl.ds(s, n), :], w_s.at[pl.ds(s, n), :], wsem.at[k]))
        w_copies[-1].start()
    mine = pl.ds(pl.multiple_of(i * half, 128), half)
    theirs = pl.ds(pl.multiple_of(other * half, 128), half)
    own_og = pltpu.make_async_copy(og.at[:, mine], og_s.at[j, i], local.at[0])
    own_og.start()
    own_rows = pl.ds(pl.multiple_of(i * tok, 128), tok)
    own_hid = pltpu.make_async_copy(hid, hid_all.at[own_rows, :], local.at[1])
    own_hid.start()

    barrier = pltpu.get_barrier_semaphore()
    for way in (X, UP, DOWN, Y, CORE):
        def greet(way=way):
            pl.semaphore_signal(barrier, inc=1, device_id=places[way],
                                device_id_type=pl.DeviceIdType.MESH)
        guarded(way, greet)
    pl.semaphore_wait(barrier, 3 + jnp.where(z < depth - 1, 1, 0) + jnp.where(z > 0, 1, 0))

    cross = pltpu.make_async_remote_copy(
        og.at[:, theirs], og_s.at[j, i], send.at[X, i, j], recv.at[i, j],
        device_id=places[X], device_id_type=pl.DeviceIdType.MESH)
    cross.start()
    step = tok // HID_PARTS
    hid_copies = []
    for k in range(HID_PARTS):
        at = pl.ds(pl.multiple_of(i * tok + k * step, 16), step)
        hid_copies.append(pltpu.make_async_remote_copy(
            hid.at[pl.ds(k * step, step), :], hid_all.at[at, :], hsend.at[k], hrecv.at[k],
            device_id=places[X], device_id_type=pl.DeviceIdType.MESH))
        hid_copies[-1].start()

    def block_copy(way, g, t):
        return pltpu.make_async_remote_copy(
            og_s.at[t, g], og_s.at[t, g], send.at[way, g, t], recv.at[g, t],
            device_id=places[way], device_id_type=pl.DeviceIdType.MESH)

    def keep(g, t):
        rows_at = pl.ds(pl.multiple_of((g * tp + t) * rows, 16), rows)
        return pltpu.make_async_copy(og_s.at[t, g], grads.at[rows_at, :], gsem.at[g, t])

    def arrived(g, t):
        block_copy(CORE, g, t).wait_recv()

    def pass_on(g, t, ways):
        for way in ways:
            guarded(way, lambda way=way: block_copy(way, g, t).start())
        keep(g, t).start()

    def hops(g):
        def own():
            pass_on(g, j, (UP, DOWN, Y, CORE))

        def along(s):
            def below():
                t = index(z - s, y, c)
                arrived(g, t)
                pass_on(g, t, (UP, Y, CORE))

            def above():
                t = index(z + s, y, c)
                arrived(g, t)
                pass_on(g, t, (DOWN, Y, CORE))

            pl.when(z - s >= 0)(below)
            pl.when(z + s < depth)(above)

        def across(s):
            def one(zz):
                t = index(zz, 1 - y, c)
                arrived(g, t)
                pass_on(g, t, (CORE,))

            if s == 0:
                one(z)
            else:
                pl.when(z - s >= 0)(lambda: one(z - s))
                pl.when(z + s < depth)(lambda: one(z + s))

        steps = [own]
        for s in range(1, depth):
            steps.append(functools.partial(along, s))
            steps.append(functools.partial(across, s - 1))
        steps.append(functools.partial(across, depth - 1))
        return steps

    near = z // (depth // 2)
    run = tp // 2

    def from_core(part):
        first = part * (depth // 2) * ROWS

        @pl.loop(0, depth // 2 * ROWS)
        def _(k):
            t = (first + k) * CORES + 1 - c
            for g in range(2):
                arrived(g, t)
                keep(g, t).start()

    def multiply(part, k):
        s = starts[k]
        n = min(WIDE, units - s)
        if waited[k] == 0:
            w_copies[k].wait()
            waited[k] = 1
        at = pl.ds(part * run, run)
        lhs = og_s[at].reshape(run * 2 * rows, half)
        v = lax.dot_general(lhs, w_s[pl.ds(s, n), :], (((1,), (1,)), ((), ())),
                            preferred_element_type=jnp.float32)
        v = v.astype(jnp.bfloat16).reshape(run, 2, rows, n)
        for g in range(2):
            pb_s[g, at, :, pl.ds(s, n)] = v[:, g]

    waited = [0] * len(starts)
    own_og.wait()
    own_steps = hops(i)
    other_steps = hops(other)
    own_steps[0]()
    arrived(other, j)
    other_steps[0]()
    cut = depth // 2 * 2 + 1
    for k in range(1, cut):
        own_steps[k]()
        other_steps[k]()
    from_core(near)
    rest = []
    for k in range(cut, len(own_steps)):
        rest += [own_steps[k], other_steps[k]]
    swaps = []
    for k in range(max(len(starts), len(rest))):
        if k < len(rest):
            rest[k]()
        if k < len(starts):
            multiply(near, k)
            n = min(WIDE, units - starts[k])
            cols = pl.ds(starts[k], n)
            swaps.append(pltpu.make_async_remote_copy(
                pb_s.at[other, pl.ds(near * run, run), :, cols], part_here.at[:, :, cols],
                psend.at[k], precv.at[k],
                device_id=places[X], device_id_type=pl.DeviceIdType.MESH))
            swaps[-1].start()
    from_core(1 - near)
    for k in range(len(starts)):
        multiply(1 - near, k)
    out_other = pltpu.make_async_copy(
        pb_s.at[other, pl.ds((1 - near) * run, run)], part_other, local.at[2])
    out_other.start()
    out_own = pltpu.make_async_copy(pb_s.at[i], part_own, local.at[3])
    out_own.start()

    cross.wait_send()
    for copy in hid_copies + swaps:
        copy.wait()

    @pl.loop(0, CORES * depth * ROWS)
    def _(t):
        for g in range(2):
            keep(g, t).wait()
    for g in (0, 1):
        @pl.loop(0, depth)
        def _(zz, g=g):
            t = index(zz, y, c)
            pl.when((zz <= z) & (z < depth - 1))(lambda: block_copy(UP, g, t).wait_send())
            pl.when((zz >= z) & (z > 0))(lambda: block_copy(DOWN, g, t).wait_send())
            block_copy(Y, g, t).wait_send()
            block_copy(CORE, g, t).wait_send()
            block_copy(CORE, g, index(zz, 1 - y, c)).wait_send()
    own_hid.wait()
    out_other.wait()
    out_own.wait()


def gather(hidden, out_grad, down_weight, tp):
    tok, units = hidden.shape
    half = down_weight.shape[1]
    rows = out_grad.shape[0]
    dma = pltpu.SemaphoreType.DMA
    pieces = pl.cdiv(units, WIDE)
    anyspace = pl.BlockSpec(memory_space=pl.ANY)
    return pl.pallas_call(
        functools.partial(gather_kernel, tp),
        out_shape=(
            jax.ShapeDtypeStruct((2 * tok, half), jnp.bfloat16),
            jax.ShapeDtypeStruct((2 * tok, units), jnp.bfloat16),
            jax.ShapeDtypeStruct((tp // 2, rows, units), jnp.bfloat16),
            jax.ShapeDtypeStruct((tp // 2, rows, units), jnp.bfloat16),
            jax.ShapeDtypeStruct((tp, rows, units), jnp.bfloat16),
        ),
        in_specs=[anyspace] * 3,
        out_specs=[anyspace] * 5,
        scratch_shapes=[
            pltpu.VMEM((tp, 2, rows, half), jnp.bfloat16),
            pltpu.VMEM((units, half), jnp.bfloat16),
            pltpu.VMEM((2, tp, rows, units), jnp.bfloat16),
            dma((5, 2, tp)),
            dma((2, tp)),
            dma((HID_PARTS,)),
            dma((HID_PARTS,)),
            dma((pieces,)),
            dma((pieces,)),
            dma((4,)),
            dma((pl.cdiv(units, WIDE),)),
            dma((2, tp)),
        ],
        compiler_params=pltpu.CompilerParams(
            collective_id=0, has_side_effects=True, vmem_limit_bytes=60 * 2**20),
    )(hidden, out_grad, down_weight)


def weight_kernel(h, g, out, ht):
    @pl.when(pl.program_id(0) == 0)
    def _():
        ht[...] = h[...].T

    out[...] = jnp.dot(ht[...], g[...], preferred_element_type=jnp.float32).astype(out.dtype)


def weight_gradient(hidden_all, grads):
    tokens, units = hidden_all.shape
    half = grads.shape[1]
    tile = TILE if half % TILE == 0 else 128
    return pl.pallas_call(
        weight_kernel,
        grid=(half // tile,),
        out_shape=jax.ShapeDtypeStruct((units, half), jnp.bfloat16),
        in_specs=[
            pl.BlockSpec((tokens, units), lambda n: (0, 0)),
            pl.BlockSpec((tokens, tile), lambda n: (0, n)),
        ],
        out_specs=pl.BlockSpec((units, tile), lambda n: (0, n)),
        scratch_shapes=[pltpu.VMEM((units, tokens), jnp.bfloat16)],
        compiler_params=pltpu.CompilerParams(vmem_limit_bytes=56 * 2**20),
        cost_estimate=pl.CostEstimate(
            flops=2 * tokens * units * half,
            bytes_accessed=2 * (tokens * (units + half) + units * half),
            transcendentals=0),
    )(hidden_all, grads)


def shards(hidden, out_grad, down_weight):
    dp = lax.axis_size("dp")
    tp = lax.axis_size("tp")
    grads, hidden_all, part_other, part_here, part_own = gather(
        hidden, out_grad, down_weight, tp)
    received = lax.ppermute(part_other, "dp", [(k, 1 - k) for k in range(dp)])
    weight_grad = weight_gradient(hidden_all, grads)
    first = lax.axis_index("tp") < tp // 2
    received = jnp.where(first, jnp.concatenate([part_here, received], axis=0),
                         jnp.concatenate([received, part_here], axis=0))
    input_grad = part_own.astype(jnp.float32) + received.astype(jnp.float32)
    input_grad = input_grad.astype(jnp.bfloat16).reshape(hidden.shape)
    return (input_grad, weight_grad)


def plain_shards(hidden, out_grad, down_weight):
    own = lax.all_to_all(out_grad, "dp", split_axis=1, concat_axis=0, tiled=True)
    dp = lax.axis_size("dp")
    own = own.reshape(dp, out_grad.shape[0], own.shape[1])
    grads = lax.all_gather(own, "tp", axis=1, tiled=True)
    grads = grads.reshape(-1, grads.shape[2])
    hidden_all = lax.all_gather(hidden, "dp", axis=0, tiled=True)
    partial = lax.dot_general(
        grads, down_weight, (((1,), (1,)), ((), ())), preferred_element_type=jnp.float32
    )
    input_grad = lax.psum_scatter(partial, "dp", scatter_dimension=0, tiled=True)
    weight_grad = lax.dot_general(
        hidden_all, grads, (((0,), (0,)), ((), ())), preferred_element_type=jnp.float32
    )
    return (input_grad.astype(jnp.bfloat16), weight_grad.astype(jnp.bfloat16))


def choose(dp, tp, hidden, out_grad, down_weight):
    def run(hidden, out_grad, down_weight):
        rows = out_grad.shape[0]
        fits = (
            dp == 2 and tp % (2 * CORES * ROWS) == 0 and rows % 16 == 0
            and hidden.shape[0] % (16 * HID_PARTS) == 0
            and hidden.shape[1] % 128 == 0 and down_weight.shape[1] % 128 == 0
        )
        return (shards if fits else plain_shards)(hidden, out_grad, down_weight)
    return run(hidden, out_grad, down_weight)


def solution(mesh):
    placed = (P("dp", "tp"), P(("dp", "tp"), None), P("tp", "dp"))
    return jax.shard_map(
        functools.partial(choose, mesh.shape["dp"], mesh.shape["tp"]),
        mesh=mesh,
        in_specs=placed,
        out_specs=(P("dp", "tp"), P("tp", "dp")),
        check_vma=False,
    )
```
